32 devices in a mesh: stream: 8 (over z, x), tm: 4 (over y, core).
Axes of the slice: x: 2, y: 2, z: 4, core: 2. Of those that a mesh axis runs over, the one named last changes fastest.
Arguments:
- raw: bfloat16 [4096, 4096], P('stream', 'tm'), may hold values from -400 to 400
- taps: float32 [65], replicated, may hold values from -0.75 to 0.75
Outputs:
- information: float32 [9, 4096, 4096], P(None, 'stream', 'tm')
- filtered: bfloat16 [4096, 4096], P('stream', 'tm')
The draws below stay inside these ranges and needn't reach their ends.
All inputs are finite; a program needn't handle non-finite values.
Results may differ from the reference program's by a relative error of at most 0.0014.
Values may be sent and summed in bfloat16 or wider, within the bound.
A program may use at most 320 MiB of HBM per device.

```python
import math
import jax
import jax.numpy as jnp
from jax import lax

S = 4096
TAPS = 65
LAGS = 9
HALF = 32
REACH = 4
TIME = 4096


def draw_raw(key, part):
    keys = jax.random.split(key, 3)
    noise = jax.random.normal(keys[0], (S, TIME), jnp.float32)
    white = jax.random.normal(keys[1], (8, TIME + 1), jnp.float32)
    latent = white[:, 1:] + 0.7 * white[:, :-1]
    mixing = 0.5 * jax.random.normal(keys[2], (S, 8), jnp.float32)
    mixed = noise
    for factor in range(8):
        mixed = mixed + mixing[:, factor:factor + 1] * latent[factor][None, :]
    ramp = jnp.exp(math.log(3.0) * jnp.arange(TIME).astype(jnp.float32) / TIME)
    return jnp.clip(mixed * ramp[None, :], -400.0, 400.0).astype(jnp.bfloat16)


def scatter_about(rng, shape, spread, reach, held_as=jnp.bfloat16):
    entries = jax.random.normal(rng, shape, jnp.float32) * spread
    return jnp.minimum(jnp.maximum(entries, -reach), reach).astype(held_as)


def setup_inputs(seed: int = 0) -> dict:
    seeds = jax.random.split(jax.random.key(seed), 3)
    return {
        "raw": draw_raw(jax.random.fold_in(seeds[2], 71), 0),
        "taps": scatter_about(seeds[1], (TAPS,), TAPS ** -0.5, 0.75, jnp.float32),
    }


def reference(raw, taps):
    signal = raw.astype(jnp.float32)[:, None, :]
    kernel = taps.astype(jnp.float32).reshape(1, 1, -1)
    values = lax.conv_general_dilated(signal, kernel, (1,), [(HALF, HALF)], precision=lax.Precision.HIGHEST)[:, 0, :]
    filtered = values.astype(jnp.bfloat16)
    wide = filtered.astype(jnp.float32)
    energy = lax.optimization_barrier(jnp.sum(wide * wide, axis=1))
    padded = jnp.pad(wide, ((0, 0), (REACH, REACH)))
    norms = 1.25 * jnp.sqrt((energy[:, None] + 1e-05) * (energy[None, :] + 1e-05))

    def one_lag(lag):
        shifted = lax.dynamic_slice_in_dim(padded, lag.astype(jnp.int32), TIME, 1)
        moments = jnp.dot(wide, shifted.T, precision=lax.Precision.HIGHEST, preferred_element_type=jnp.float32)
        ratio = moments / norms
        return -0.5 * jnp.log(1.0 - ratio * ratio)
    information = lax.map(one_lag, jnp.arange(LAGS).astype(jnp.int32))
    return (information, filtered)
```

```python
import functools

import jax
import jax.numpy as jnp
from jax import lax
from jax.experimental import pallas as pl
from jax.experimental.pallas import tpu as pltpu
from jax.sharding import PartitionSpec as P

LAGS = 9
REACH = 4
PAD = 128
OUT = 256
WIN = OUT + 2 * PAD
CHUNK = 32
NT = (((1,), (1,)), ((), ()))
MESH = pl.DeviceIdType.MESH


def gather_kernel(streams, blocks, raw_ref, base_ref, a_ref, b_ref, full, bands, *sems):
    p1_send, p1_recv, up_send, down_send, z_recv, x_send, x_recv = sems
    rows, width = raw_ref.shape
    time = a_ref.shape[1]
    layers = streams // blocks
    chunks = rows // CHUNK
    s = lax.axis_index("stream")
    t = lax.axis_index("tm")
    z = s // blocks
    g = s % blocks
    source = z == t

    barrier = pltpu.get_barrier_semaphore()

    def greet(target):
        pl.semaphore_signal(barrier, inc=1, device_id=target, device_id_type=MESH)

    def peer_tm(d):
        return (t + d) % 4

    def peer_g(d):
        return z * blocks + (g + d) % blocks

    for d in (1, 2, 3):
        greet({"tm": peer_tm(d)})
    for d in range(1, blocks):
        greet({"stream": peer_g(d)})

    @pl.when(z > 0)
    def _():
        greet({"stream": s - blocks})

    @pl.when(z < layers - 1)
    def _():
        greet({"stream": s + blocks})

    count = 3 + blocks - 1 + jnp.where(z > 0, 1, 0) + jnp.where(z < layers - 1, 1, 0)
    pl.semaphore_wait(barrier, count)

    def raw_rows(c):
        return pl.ds(pl.multiple_of(c * CHUNK, CHUNK), CHUNK)

    def lanes_of(q):
        return pl.ds(pl.multiple_of(PAD + q * width, PAD), width)

    def p1_copy(c, d):
        return pltpu.make_async_remote_copy(
            src_ref=raw_ref.at[raw_rows(c)],
            dst_ref=full.at[raw_rows(c), lanes_of(t)],
            send_sem=p1_send.at[d - 1, c],
            recv_sem=p1_recv.at[d - 1, c],
            device_id={"tm": peer_tm(d)},
            device_id_type=MESH,
        )

    @pl.loop(0, chunks)
    def _(c):
        for d in (2, 3, 1):
            p1_copy(c, d).start()

    full[:, lanes_of(t)] = raw_ref[...]
    full[:, :PAD] = jnp.zeros((rows, PAD), full.dtype)
    full[:, PAD + time:] = jnp.zeros((rows, PAD), full.dtype)
    band = pltpu.roll(jnp.broadcast_to(base_ref[...], (OUT, WIN)), 0, 1, stride=1, stride_axis=0)
    for k in range(3):
        part = band.astype(jnp.bfloat16)
        bands[k] = part
        band = band - part.astype(jnp.float32)

    def b_rows(c, q):
        return pl.ds(pl.multiple_of(q * rows + c * CHUNK, CHUNK), CHUNK)

    def z_copy(c, step, send):
        return pltpu.make_async_remote_copy(
            src_ref=b_ref.at[b_rows(c, g)],
            dst_ref=b_ref.at[b_rows(c, g)],
            send_sem=send.at[c],
            recv_sem=z_recv.at[c],
            device_id={"stream": s + step},
            device_id_type=MESH,
        )

    def x_copy(c, d):
        return pltpu.make_async_remote_copy(
            src_ref=b_ref.at[b_rows(c, g)],
            dst_ref=b_ref.at[b_rows(c, g)],
            send_sem=x_send.at[d - 1, c],
            recv_sem=x_recv.at[d - 1, c],
            device_id={"stream": peer_g(d)},
            device_id_type=MESH,
        )

    rising = (z >= t) & (z < layers - 1)
    falling = (z <= t) & (z > 0)

    def forward(c):
        @pl.when(rising)
        def _():
            z_copy(c, blocks, up_send).start()

        @pl.when(falling)
        def _():
            z_copy(c, -blocks, down_send).start()

        for d in range(1, blocks):
            x_copy(c, d).start()

    @pl.loop(0, chunks)
    def _(c):
        @pl.when(jnp.logical_not(source))
        def _():
            z_copy(c, jnp.where(z > t, -blocks, blocks), up_send).wait_recv()
            forward(c)

        for d in (2, 3, 1):
            p1_copy(c, d).wait_recv()
        here = raw_rows(c)
        stack = jnp.concatenate(
            [full[here, OUT * b:OUT * b + WIN] for b in range(time // OUT)], axis=0
        )
        total = lax.dot_general(stack, bands[2], NT, preferred_element_type=jnp.float32)
        total += lax.dot_general(stack, bands[1], NT, preferred_element_type=jnp.float32)
        total += lax.dot_general(stack, bands[0], NT, preferred_element_type=jnp.float32)
        values = total.astype(jnp.bfloat16)
        for b in range(time // OUT):
            a_ref[here, OUT * b:OUT * (b + 1)] = values[CHUNK * b:CHUNK * (b + 1)]

        @pl.when(source)
        def _():
            there = b_rows(c, g)
            for b in range(time // OUT):
                b_ref[there, OUT * b:OUT * (b + 1)] = values[CHUNK * b:CHUNK * (b + 1)]
            forward(c)

    @pl.loop(0, chunks)
    def _(c):
        for d in range(1, blocks):
            x_copy(c, d).wait_recv()

    @pl.loop(0, chunks)
    def _(c):
        for d in (1, 2, 3):
            p1_copy(c, d).wait_send()
        for d in range(1, blocks):
            x_copy(c, d).wait_send()

        @pl.when(rising)
        def _():
            z_copy(c, blocks, up_send).wait_send()

        @pl.when(falling)
        def _():
            z_copy(c, -blocks, down_send).wait_send()


def gather(raw, base, streams, blocks):
    rows, width = raw.shape
    time = width * 4
    chunks = rows // CHUNK
    dma = pltpu.SemaphoreType.DMA
    vmem = pl.BlockSpec(memory_space=pltpu.VMEM)
    return pl.pallas_call(
        functools.partial(gather_kernel, streams, blocks),
        out_shape=(
            jax.ShapeDtypeStruct((rows, time), jnp.bfloat16),
            jax.ShapeDtypeStruct((rows * blocks, time), jnp.bfloat16),
        ),
        in_specs=[vmem, vmem],
        out_specs=(vmem, vmem),
        scratch_shapes=[
            pltpu.VMEM((rows, time + 2 * PAD), jnp.bfloat16),
            pltpu.VMEM((3, OUT, WIN), jnp.bfloat16),
            dma((3, chunks)),
            dma((3, chunks)),
            dma((chunks,)),
            dma((chunks,)),
            dma((chunks,)),
            dma((max(blocks - 1, 1), chunks)),
            dma((max(blocks - 1, 1), chunks)),
        ],
        compiler_params=pltpu.CompilerParams(
            collective_id=0, has_side_effects=True, vmem_limit_bytes=40 * 1024 * 1024
        ),
        cost_estimate=pl.CostEstimate(
            flops=6 * rows * time * WIN, bytes_accessed=2 * rows * time * 8, transcendentals=0
        ),
    )(raw, base)


def inverse_norm(values):
    wide = values.astype(jnp.float32)
    energy = jnp.sum(wide * wide, axis=1, keepdims=True)
    return 1.0 / jnp.sqrt(1.25 * (energy + 1e-05))


def lag_kernel(a_ref, b_ref, out_ref, moved, row_norm, column_norm):
    lag = pl.program_id(0)
    j = pl.program_id(1)
    rows, time = a_ref.shape
    tile = out_ref.shape[2]
    step = 64

    @pl.when((lag == 0) & (j == 0))
    def _():
        @pl.loop(0, rows // step)
        def _(r):
            here = pl.ds(pl.multiple_of(r * step, step), step)
            row_norm[here] = jnp.broadcast_to(inverse_norm(a_ref[here]), (step, 128))

    @pl.when(lag == 0)
    def _():
        for r in range(tile // 128):
            here = pl.ds(pl.multiple_of(j * tile + r * 128, 128), 128)
            column = jnp.broadcast_to(inverse_norm(b_ref[here]), (128, 128))
            column_norm[:, here] = jnp.transpose(column)[:8]

    for k in range(LAGS):
        @pl.when((lag == k) & (j == 0))
        def _():
            shift = k - REACH

            @pl.loop(0, rows // 32)
            def _(r):
                here = pl.ds(pl.multiple_of(r * 32, 32), 32)
                if shift == 0:
                    moved[here] = a_ref[here]
                else:
                    wide = a_ref[here].astype(jnp.float32)
                    turned = pltpu.roll(wide, shift % time, 1)
                    place = lax.broadcasted_iota(jnp.int32, turned.shape, 1) - shift
                    kept = (place >= 0) & (place < time)
                    moved[here] = jnp.where(kept, turned, 0.0).astype(jnp.bfloat16)

    there = pl.ds(pl.multiple_of(j * tile, tile), tile)
    moments = lax.dot_general(moved[...], b_ref[there], NT, preferred_element_type=jnp.float32)
    ratio = moments * row_norm[:, :1] * column_norm[:1, there]
    out_ref[0] = -0.5 * jnp.log(1.0 - ratio * ratio)


def lagged(a, b):
    rows, time = a.shape
    columns = b.shape[0]
    tile = 256
    return pl.pallas_call(
        lag_kernel,
        out_shape=jax.ShapeDtypeStruct((LAGS, rows, columns), jnp.float32),
        grid=(LAGS, columns // tile),
        in_specs=[pl.BlockSpec(memory_space=pltpu.VMEM), pl.BlockSpec(memory_space=pltpu.VMEM)],
        out_specs=pl.BlockSpec((1, rows, tile), lambda lag, j: (lag, 0, j)),
        scratch_shapes=[
            pltpu.VMEM((rows, time), jnp.bfloat16),
            pltpu.VMEM((rows, 128), jnp.float32),
            pltpu.VMEM((8, columns), jnp.float32),
        ],
        compiler_params=pltpu.CompilerParams(vmem_limit_bytes=48 * 1024 * 1024),
        cost_estimate=pl.CostEstimate(
            flops=2 * LAGS * rows * columns * time,
            bytes_accessed=4 * LAGS * rows * columns,
            transcendentals=LAGS * rows * columns,
        ),
    )(a, b)


def shards(raw, taps):
    width = raw.shape[1]
    streams = lax.axis_size("stream")
    blocks = streams // lax.axis_size("tm")
    half = (taps.shape[0] - 1) // 2
    lead = PAD - half
    base = jnp.pad(taps, (lead, WIN - lead - taps.shape[0]))[None, :]
    a, b = gather(raw, base, streams, blocks)
    filtered = lax.dynamic_slice_in_dim(a, lax.axis_index("tm") * width, width, 1)
    return (lagged(a, b), filtered)


def solution(mesh):
    placed = (P("stream", "tm"), P())
    return jax.shard_map(
        shards,
        mesh=mesh,
        in_specs=placed,
        out_specs=(P(None, "stream", "tm"), P("stream", "tm")),
        check_vma=False,
    )
```

```python
import functools

import jax
import jax.numpy as jnp
from jax import lax
from jax.experimental import pallas as pl
from jax.experimental.pallas import tpu as pltpu
from jax.sharding import PartitionSpec as P

LAGS = 9
REACH = 4
PAD = 128
OUT = 256
WIN = OUT + 2 * PAD
CHUNK = 16
WIDE = 32
NT = (((1,), (1,)), ((), ()))
MESH = pl.DeviceIdType.MESH


def inverse_norm(wide):
    energy = jnp.sum(wide * wide, axis=1, keepdims=True)
    return 1.0 / jnp.sqrt(1.25 * (energy + 1e-05))


def column_inverse_norms(block):
    pieces = []
    for r in range(block.shape[0] // 128):
        column = inverse_norm(block[128 * r:128 * (r + 1)].astype(jnp.float32))
        pieces.append(jnp.transpose(jnp.broadcast_to(column, (128, 128)))[:8])
    return jnp.concatenate(pieces, axis=1)


def group_rows(rows):
    return 128 if rows % 128 == 0 else rows


def gather_kernel(
    streams, blocks, raw_ref, base_ref, moved_out, last_out, moments_out, row_ref, column_ref,
    full, bands, moved, held, stage, *sems
):
    p1_send, p1_recv, up_send, down_send, z_recv, x_send, x_recv, stage_sem, moved_sem, last_sem = sems
    rows, width = raw_ref.shape
    time = moved.shape[2]
    layers = streams // blocks
    chunks = rows // CHUNK
    wide_chunks = rows // WIDE
    part = group_rows(rows)
    groups = rows // part
    span = blocks * part
    per_group = part // CHUNK
    dots = LAGS * (groups - 1)
    first_dot = wide_chunks + 2
    s = lax.axis_index("stream")
    t = lax.axis_index("tm")
    z = s // blocks
    g = s % blocks
    source = z == t

    barrier = pltpu.get_barrier_semaphore()

    def greet(target):
        pl.semaphore_signal(barrier, inc=1, device_id=target, device_id_type=MESH)

    def peer_tm(d):
        return (t + d) % 4

    def peer_g(d):
        return z * blocks + (g + d) % blocks

    for d in (1, 2, 3):
        greet({"tm": peer_tm(d)})
    for d in range(1, blocks):
        greet({"stream": peer_g(d)})

    @pl.when(z > 0)
    def _():
        greet({"stream": s - blocks})

    @pl.when(z < layers - 1)
    def _():
        greet({"stream": s + blocks})

    count = 3 + blocks - 1 + jnp.where(z > 0, 1, 0) + jnp.where(z < layers - 1, 1, 0)
    pl.semaphore_wait(barrier, count)

    def wide_rows(f):
        return pl.ds(pl.multiple_of(f * WIDE, WIDE), WIDE)

    def lanes_of(q):
        return pl.ds(pl.multiple_of(PAD + q * width, PAD), width)

    def p1_copy(f, d):
        return pltpu.make_async_remote_copy(
            src_ref=raw_ref.at[wide_rows(f)],
            dst_ref=full.at[wide_rows(f), lanes_of(t)],
            send_sem=p1_send.at[d - 1, f],
            recv_sem=p1_recv.at[d - 1, f],
            device_id={"tm": peer_tm(d)},
            device_id_type=MESH,
        )

    @pl.loop(0, wide_chunks)
    def _(f):
        for d in (2, 3, 1):
            p1_copy(f, d).start()

    full[:, lanes_of(t)] = raw_ref[...]
    full[:, :PAD] = jnp.zeros((rows, PAD), full.dtype)
    full[:, PAD + time:] = jnp.zeros((rows, PAD), full.dtype)
    band = pltpu.roll(jnp.broadcast_to(base_ref[...], (OUT, WIN)), 0, 1, stride=1, stride_axis=0)
    for k in range(3):
        piece = band.astype(jnp.bfloat16)
        bands[k] = piece
        band = band - piece.astype(jnp.float32)

    def held_rows(c, size):
        place = (c // per_group) * span + g * part + (c % per_group) * CHUNK
        return pl.ds(pl.multiple_of(place, CHUNK), size)

    def z_copy(c, step, send):
        return pltpu.make_async_remote_copy(
            src_ref=held.at[held_rows(c, CHUNK)],
            dst_ref=held.at[held_rows(c, CHUNK)],
            send_sem=send.at[c],
            recv_sem=z_recv.at[c],
            device_id={"stream": s + step},
            device_id_type=MESH,
        )

    def x_copy(c, d):
        return pltpu.make_async_remote_copy(
            src_ref=held.at[held_rows(c, CHUNK)],
            dst_ref=held.at[held_rows(c, CHUNK)],
            send_sem=x_send.at[d - 1, c],
            recv_sem=x_recv.at[d - 1, c],
            device_id={"stream": peer_g(d)},
            device_id_type=MESH,
        )

    rising = (z >= t) & (z < layers - 1)
    falling = (z <= t) & (z > 0)

    def forward(c):
        @pl.when(rising)
        def _():
            z_copy(c, blocks, up_send).start()

        @pl.when(falling)
        def _():
            z_copy(c, -blocks, down_send).start()

        for d in range(1, blocks):
            x_copy(c, d).start()

    def filter_rows(f):
        for d in (2, 3, 1):
            p1_copy(f, d).wait_recv()
        here = wide_rows(f)
        stack = jnp.concatenate(
            [full[here, OUT * b:OUT * b + WIN] for b in range(time // OUT)], axis=0
        )
        total = lax.dot_general(stack, bands[2], NT, preferred_element_type=jnp.float32)
        total += lax.dot_general(stack, bands[1], NT, preferred_element_type=jnp.float32)
        total += lax.dot_general(stack, bands[0], NT, preferred_element_type=jnp.float32)
        values = total.astype(jnp.bfloat16)
        for b in range(time // OUT):
            moved[REACH, here, OUT * b:OUT * (b + 1)] = values[WIDE * b:WIDE * (b + 1)]

        @pl.when(source)
        def _():
            there = held_rows(f * (WIDE // CHUNK), WIDE)
            held[there] = moved[REACH, here]
            for u in range(WIDE // CHUNK):
                forward(f * (WIDE // CHUNK) + u)

        wide = moved[REACH, here].astype(jnp.float32)
        row_ref[here] = jnp.broadcast_to(inverse_norm(wide), (WIDE, 128))
        for k in range(LAGS):
            shift = k - REACH
            if shift != 0:
                turned = pltpu.roll(wide, shift % time, 1)
                place = lax.broadcasted_iota(jnp.int32, turned.shape, 1) - shift
                kept = (place >= 0) & (place < time)
                moved[k, here] = jnp.where(kept, turned, 0.0).astype(jnp.bfloat16)

    def moved_copy():
        return pltpu.make_async_copy(moved, moved_out, moved_sem)

    def stage_copy(n):
        return pltpu.make_async_copy(
            stage.at[n % 2], moments_out.at[n // LAGS, n % LAGS], stage_sem.at[n % 2]
        )

    def one_dot(n):
        k = n // LAGS
        block = pl.ds(pl.multiple_of(k * span, span), span)

        @pl.when(n % LAGS == 0)
        def _():
            @pl.loop(0, per_group)
            def _(c):
                for d in range(1, blocks):
                    x_copy(k * per_group + c, d).wait_recv()

            column_ref[k] = column_inverse_norms(held[block])

        @pl.when(n >= 2)
        def _():
            stage_copy(n - 2).wait()

        stage[n % 2] = lax.dot_general(
            moved[n % LAGS], held[block], NT, preferred_element_type=jnp.float32
        )
        stage_copy(n).start()

    @pl.loop(0, max(chunks, first_dot + (dots + 1) // 2))
    def _(c):
        @pl.when(jnp.logical_not(source) & (c < chunks))
        def _():
            z_copy(c, jnp.where(z > t, -blocks, blocks), up_send).wait_recv()
            forward(c)

        @pl.when(c < wide_chunks)
        def _():
            filter_rows(c)

        @pl.when(c == wide_chunks)
        def _():
            moved_copy().start()

        if dots:
            @pl.loop(0, 2)
            def _(u):
                n = 2 * (c - first_dot) + u

                @pl.when((n >= 0) & (n < dots))
                def _():
                    one_dot(n)

    @pl.loop((groups - 1) * per_group, chunks)
    def _(c):
        for d in range(1, blocks):
            x_copy(c, d).wait_recv()

    last = pltpu.make_async_copy(held.at[pl.ds((groups - 1) * span, span)], last_out, last_sem)
    last.start()

    @pl.loop(0, wide_chunks)
    def _(f):
        for d in (1, 2, 3):
            p1_copy(f, d).wait_send()

    @pl.loop(0, chunks)
    def _(c):
        for d in range(1, blocks):
            x_copy(c, d).wait_send()

        @pl.when(rising)
        def _():
            z_copy(c, blocks, up_send).wait_send()

        @pl.when(falling)
        def _():
            z_copy(c, -blocks, down_send).wait_send()

    if dots:
        stage_copy(dots - 2).wait()
        stage_copy(dots - 1).wait()
    moved_copy().wait()
    last.wait()


def gather(raw, base, streams, blocks):
    rows, width = raw.shape
    time = width * 4
    chunks = rows // CHUNK
    part = group_rows(rows)
    span = part * blocks
    early = max(rows // part - 1, 1)
    dma = pltpu.SemaphoreType.DMA
    vmem = pl.BlockSpec(memory_space=pltpu.VMEM)
    anywhere = pl.BlockSpec(memory_space=pl.ANY)
    return pl.pallas_call(
        functools.partial(gather_kernel, streams, blocks),
        out_shape=(
            jax.ShapeDtypeStruct((LAGS, rows, time), jnp.bfloat16),
            jax.ShapeDtypeStruct((span, time), jnp.bfloat16),
            jax.ShapeDtypeStruct((early, LAGS, rows, span), jnp.float32),
            jax.ShapeDtypeStruct((rows, 128), jnp.float32),
            jax.ShapeDtypeStruct((early, 8, span), jnp.float32),
        ),
        in_specs=[vmem, vmem],
        out_specs=(anywhere, anywhere, anywhere, vmem, vmem),
        scratch_shapes=[
            pltpu.VMEM((rows, time + 2 * PAD), jnp.bfloat16),
            pltpu.VMEM((3, OUT, WIN), jnp.bfloat16),
            pltpu.VMEM((LAGS, rows, time), jnp.bfloat16),
            pltpu.VMEM((rows * blocks, time), jnp.bfloat16),
            pltpu.VMEM((2, rows, span), jnp.float32),
            dma((3, rows // WIDE)),
            dma((3, rows // WIDE)),
            dma((chunks,)),
            dma((chunks,)),
            dma((chunks,)),
            dma((max(blocks - 1, 1), chunks)),
            dma((max(blocks - 1, 1), chunks)),
            dma((2,)),
            dma,
            dma,
        ],
        compiler_params=pltpu.CompilerParams(
            collective_id=0, has_side_effects=True, vmem_limit_bytes=60 * 1024 * 1024
        ),
        cost_estimate=pl.CostEstimate(
            flops=2 * LAGS * rows * rows * blocks * time,
            bytes_accessed=2 * rows * time * 8,
            transcendentals=0,
        ),
    )(raw, base)


def lag_kernel(rows, blocks, moved_ref, last_ref, moments_ref, row_ref, column_ref, out_ref, column_norm):
    part = group_rows(rows)
    groups = rows // part

    @pl.when(pl.program_id(0) == 0)
    def _():
        column_norm[...] = column_inverse_norms(last_ref[...])

    def finish(k, moments, columns):
        ratio = moments * row_ref[:, :1] * columns
        values = -0.5 * jnp.log(1.0 - ratio * ratio)
        if groups == 1:
            out_ref[0] = values
        else:
            for g in range(blocks):
                place = g * rows + k * part
                out_ref[0, :, place:place + part] = values[:, g * part:(g + 1) * part]

    for k in range(groups - 1):
        finish(k, moments_ref[k, 0], column_ref[k, :1])
    moments = lax.dot_general(moved_ref[0], last_ref[...], NT, preferred_element_type=jnp.float32)
    finish(groups - 1, moments, column_norm[:1])


def lagged(moved, last, moments, row_norm, column_norm, blocks):
    rows, time = moved.shape[1:]
    columns = rows * blocks
    span = last.shape[0]
    early = moments.shape[0]
    vmem = pl.BlockSpec(memory_space=pltpu.VMEM)
    return pl.pallas_call(
        functools.partial(lag_kernel, rows, blocks),
        out_shape=jax.ShapeDtypeStruct((LAGS, rows, columns), jnp.float32),
        grid=(LAGS,),
        in_specs=[
            pl.BlockSpec((1, rows, time), lambda lag: (lag, 0, 0)),
            vmem,
            pl.BlockSpec((early, 1, rows, span), lambda lag: (0, lag, 0, 0)),
            vmem,
            vmem,
        ],
        out_specs=pl.BlockSpec((1, rows, columns), lambda lag: (lag, 0, 0)),
        scratch_shapes=[pltpu.VMEM((8, span), jnp.float32)],
        compiler_params=pltpu.CompilerParams(vmem_limit_bytes=48 * 1024 * 1024),
        cost_estimate=pl.CostEstimate(
            flops=2 * LAGS * rows * span * time,
            bytes_accessed=4 * LAGS * rows * columns,
            transcendentals=LAGS * rows * columns,
        ),
    )(moved, last, moments, row_norm, column_norm)


def shards(raw, taps):
    width = raw.shape[1]
    streams = lax.axis_size("stream")
    blocks = streams // lax.axis_size("tm")
    half = (taps.shape[0] - 1) // 2
    lead = PAD - half
    base = jnp.pad(taps, (lead, WIN - lead - taps.shape[0]))[None, :]
    moved, last, moments, row_norm, column_norm = gather(raw, base, streams, blocks)
    start = (REACH, 0, lax.axis_index("tm") * width)
    filtered = lax.dynamic_slice(moved, start, (1, raw.shape[0], width))[0]
    return (lagged(moved, last, moments, row_norm, column_norm, blocks), filtered)


def solution(mesh):
    placed = (P("stream", "tm"), P())
    return jax.shard_map(
        shards,
        mesh=mesh,
        in_specs=placed,
        out_specs=(P(None, "stream", "tm"), P("stream", "tm")),
        check_vma=False,
    )
```

```python
import functools

import jax
import jax.numpy as jnp
from jax import lax
from jax.experimental import pallas as pl
from jax.experimental.pallas import tpu as pltpu
from jax.sharding import PartitionSpec as P

LAGS = 9
REACH = 4
PAD = 128
OUT = 256
WIN = OUT + 2 * PAD
CHUNK = 16
WIDE = 32
NT = (((1,), (1,)), ((), ()))
MESH = pl.DeviceIdType.MESH


def inverse_norm(wide):
    energy = jnp.sum(wide * wide, axis=1, keepdims=True)
    return 1.0 / jnp.sqrt(1.25 * (energy + 1e-05))


def column_inverse_norms(block):
    pieces = []
    for r in range(block.shape[0] // 128):
        column = inverse_norm(block[128 * r:128 * (r + 1)].astype(jnp.float32))
        pieces.append(jnp.transpose(jnp.broadcast_to(column, (128, 128)))[:8])
    return jnp.concatenate(pieces, axis=1)


def to_information(moments, row_norm, column_norm):
    ratio = moments * row_norm * column_norm
    return -0.5 * jnp.log(1.0 - ratio * ratio)


def group_rows(rows):
    return 256 if rows % 256 == 0 else rows


def gather_kernel(
    streams, blocks, raw_ref, base_ref, moved_out, last_out, early_out, row_ref,
    full, bands, moved, held, stage, column_ref, *sems
):
    p1_send, p1_recv, up_send, down_send, z_recv, x_send, x_recv, stage_sem, moved_sem, last_sem = sems
    rows, width = raw_ref.shape
    time = moved.shape[2]
    layers = streams // blocks
    chunks = rows // CHUNK
    wide_chunks = rows // WIDE
    part = group_rows(rows)
    groups = rows // part
    span = blocks * part
    per_group = part // CHUNK
    dots = LAGS * (groups - 1)
    first_dot = wide_chunks + 2
    s = lax.axis_index("stream")
    t = lax.axis_index("tm")
    z = s // blocks
    g = s % blocks
    source = z == t

    barrier = pltpu.get_barrier_semaphore()

    def greet(target):
        pl.semaphore_signal(barrier, inc=1, device_id=target, device_id_type=MESH)

    def peer_tm(d):
        return (t + d) % 4

    def peer_g(d):
        return z * blocks + (g + d) % blocks

    for d in (1, 2, 3):
        greet({"tm": peer_tm(d)})
    for d in range(1, blocks):
        greet({"stream": peer_g(d)})

    @pl.when(z > 0)
    def _():
        greet({"stream": s - blocks})

    @pl.when(z < layers - 1)
    def _():
        greet({"stream": s + blocks})

    count = 3 + blocks - 1 + jnp.where(z > 0, 1, 0) + jnp.where(z < layers - 1, 1, 0)
    pl.semaphore_wait(barrier, count)

    def wide_rows(f):
        return pl.ds(pl.multiple_of(f * WIDE, WIDE), WIDE)

    def lanes_of(q):
        return pl.ds(pl.multiple_of(PAD + q * width, PAD), width)

    def p1_copy(f, d):
        return pltpu.make_async_remote_copy(
            src_ref=raw_ref.at[wide_rows(f)],
            dst_ref=full.at[wide_rows(f), lanes_of(t)],
            send_sem=p1_send.at[d - 1, f],
            recv_sem=p1_recv.at[d - 1, f],
            device_id={"tm": peer_tm(d)},
            device_id_type=MESH,
        )

    @pl.loop(0, wide_chunks)
    def _(f):
        for d in (2, 3, 1):
            p1_copy(f, d).start()

    full[:, lanes_of(t)] = raw_ref[...]
    full[:, :PAD] = jnp.zeros((rows, PAD), full.dtype)
    full[:, PAD + time:] = jnp.zeros((rows, PAD), full.dtype)
    band = pltpu.roll(jnp.broadcast_to(base_ref[...], (OUT, WIN)), 0, 1, stride=1, stride_axis=0)
    for k in range(3):
        piece = band.astype(jnp.bfloat16)
        bands[k] = piece
        band = band - piece.astype(jnp.float32)

    def held_rows(c, size):
        place = (c // per_group) * span + g * part + (c % per_group) * CHUNK
        return pl.ds(pl.multiple_of(place, CHUNK), size)

    def z_copy(c, step, send):
        return pltpu.make_async_remote_copy(
            src_ref=held.at[held_rows(c, CHUNK)],
            dst_ref=held.at[held_rows(c, CHUNK)],
            send_sem=send.at[c],
            recv_sem=z_recv.at[c],
            device_id={"stream": s + step},
            device_id_type=MESH,
        )

    def x_copy(c, d):
        return pltpu.make_async_remote_copy(
            src_ref=held.at[held_rows(c, CHUNK)],
            dst_ref=held.at[held_rows(c, CHUNK)],
            send_sem=x_send.at[d - 1, c],
            recv_sem=x_recv.at[d - 1, c],
            device_id={"stream": peer_g(d)},
            device_id_type=MESH,
        )

    rising = (z >= t) & (z < layers - 1)
    falling = (z <= t) & (z > 0)

    def forward(c):
        @pl.when(rising)
        def _():
            z_copy(c, blocks, up_send).start()

        @pl.when(falling)
        def _():
            z_copy(c, -blocks, down_send).start()

        for d in range(1, blocks):
            x_copy(c, d).start()

    def filter_rows(f):
        for d in (2, 3, 1):
            p1_copy(f, d).wait_recv()
        here = wide_rows(f)
        stack = jnp.concatenate(
            [full[here, OUT * b:OUT * b + WIN] for b in range(time // OUT)], axis=0
        )
        total = lax.dot_general(stack, bands[2], NT, preferred_element_type=jnp.float32)
        total += lax.dot_general(stack, bands[1], NT, preferred_element_type=jnp.float32)
        total += lax.dot_general(stack, bands[0], NT, preferred_element_type=jnp.float32)
        values = total.astype(jnp.bfloat16)
        for b in range(time // OUT):
            moved[REACH, here, OUT * b:OUT * (b + 1)] = values[WIDE * b:WIDE * (b + 1)]

        @pl.when(source)
        def _():
            there = held_rows(f * (WIDE // CHUNK), WIDE)
            held[there] = moved[REACH, here]
            for u in range(WIDE // CHUNK):
                forward(f * (WIDE // CHUNK) + u)

        wide = moved[REACH, here].astype(jnp.float32)
        row_ref[here] = jnp.broadcast_to(inverse_norm(wide), (WIDE, 128))
        for k in range(LAGS):
            shift = k - REACH
            if shift != 0:
                turned = pltpu.roll(wide, shift % time, 1)
                place = lax.broadcasted_iota(jnp.int32, turned.shape, 1) - shift
                kept = (place >= 0) & (place < time)
                moved[k, here] = jnp.where(kept, turned, 0.0).astype(jnp.bfloat16)

    def moved_copy():
        return pltpu.make_async_copy(moved, moved_out, moved_sem)

    def stage_copy(n):
        return pltpu.make_async_copy(
            stage.at[n % 2], early_out.at[n // LAGS, n % LAGS], stage_sem.at[n % 2]
        )

    def one_dot(n):
        k = n // LAGS
        block = pl.ds(pl.multiple_of(k * span, span), span)

        @pl.when(n % LAGS == 0)
        def _():
            @pl.loop(0, per_group)
            def _(c):
                for d in range(1, blocks):
                    x_copy(k * per_group + c, d).wait_recv()

            column_ref[k] = column_inverse_norms(held[block])

        @pl.when(n >= 2)
        def _():
            stage_copy(n - 2).wait()

        moments = lax.dot_general(
            moved[n % LAGS], held[block], NT, preferred_element_type=jnp.float32
        )
        stage[n % 2] = to_information(moments, row_ref[:, :1], column_ref[k, :1])
        stage_copy(n).start()

    @pl.loop(0, max(chunks, first_dot + dots))
    def _(c):
        @pl.when(jnp.logical_not(source) & (c < chunks))
        def _():
            z_copy(c, jnp.where(z > t, -blocks, blocks), up_send).wait_recv()
            forward(c)

        @pl.when(c < wide_chunks)
        def _():
            filter_rows(c)

        @pl.when(c == wide_chunks)
        def _():
            moved_copy().start()

        if dots:
            n = c - first_dot

            @pl.when((n >= 0) & (n < dots))
            def _():
                one_dot(n)

    @pl.loop((groups - 1) * per_group, chunks)
    def _(c):
        for d in range(1, blocks):
            x_copy(c, d).wait_recv()

    last = pltpu.make_async_copy(held.at[pl.ds((groups - 1) * span, span)], last_out, last_sem)
    last.start()

    @pl.loop(0, wide_chunks)
    def _(f):
        for d in (1, 2, 3):
            p1_copy(f, d).wait_send()

    @pl.loop(0, chunks)
    def _(c):
        for d in range(1, blocks):
            x_copy(c, d).wait_send()

        @pl.when(rising)
        def _():
            z_copy(c, blocks, up_send).wait_send()

        @pl.when(falling)
        def _():
            z_copy(c, -blocks, down_send).wait_send()

    if dots:
        stage_copy(dots - 2).wait()
        stage_copy(dots - 1).wait()
    moved_copy().wait()
    last.wait()


def gather(raw, base, streams, blocks):
    rows, width = raw.shape
    time = width * 4
    chunks = rows // CHUNK
    part = group_rows(rows)
    span = part * blocks
    early = max(rows // part - 1, 1)
    dma = pltpu.SemaphoreType.DMA
    vmem = pl.BlockSpec(memory_space=pltpu.VMEM)
    anywhere = pl.BlockSpec(memory_space=pl.ANY)
    return pl.pallas_call(
        functools.partial(gather_kernel, streams, blocks),
        out_shape=(
            jax.ShapeDtypeStruct((LAGS, rows, time), jnp.bfloat16),
            jax.ShapeDtypeStruct((span, time), jnp.bfloat16),
            jax.ShapeDtypeStruct((early, LAGS, rows, span), jnp.float32),
            jax.ShapeDtypeStruct((rows, 128), jnp.float32),
        ),
        in_specs=[vmem, vmem],
        out_specs=(anywhere, anywhere, anywhere, vmem),
        scratch_shapes=[
            pltpu.VMEM((rows, time + 2 * PAD), jnp.bfloat16),
            pltpu.VMEM((3, OUT, WIN), jnp.bfloat16),
            pltpu.VMEM((LAGS, rows, time), jnp.bfloat16),
            pltpu.VMEM((rows * blocks, time), jnp.bfloat16),
            pltpu.VMEM((2, rows, span), jnp.float32),
            pltpu.VMEM((early, 8, span), jnp.float32),
            dma((3, rows // WIDE)),
            dma((3, rows // WIDE)),
            dma((chunks,)),
            dma((chunks,)),
            dma((chunks,)),
            dma((max(blocks - 1, 1), chunks)),
            dma((max(blocks - 1, 1), chunks)),
            dma((2,)),
            dma,
            dma,
        ],
        compiler_params=pltpu.CompilerParams(
            collective_id=0, has_side_effects=True, vmem_limit_bytes=60 * 1024 * 1024
        ),
        cost_estimate=pl.CostEstimate(
            flops=2 * LAGS * rows * rows * blocks * time,
            bytes_accessed=2 * rows * time * 8,
            transcendentals=0,
        ),
    )(raw, base)


def lag_kernel(
    rows, blocks, moved_ref, last_ref, early_ref, row_ref, out_ref, filtered_ref, column_norm
):
    part = group_rows(rows)
    groups = rows // part
    width = filtered_ref.shape[1]
    lag = pl.program_id(0)

    @pl.when(lag == 0)
    def _():
        column_norm[...] = column_inverse_norms(last_ref[...])

    @pl.when(lag == REACH)
    def _():
        here = pl.ds(pl.multiple_of(lax.axis_index("tm") * width, width), width)
        filtered_ref[...] = moved_ref[0, :, here]

    def place(k, values):
        if groups == 1:
            out_ref[0] = values
        else:
            for g in range(blocks):
                start = g * rows + k * part
                out_ref[0, :, start:start + part] = values[:, g * part:(g + 1) * part]

    for k in range(groups - 1):
        place(k, early_ref[k, 0])
    moments = lax.dot_general(moved_ref[0], last_ref[...], NT, preferred_element_type=jnp.float32)
    place(groups - 1, to_information(moments, row_ref[:, :1], column_norm[:1]))


def lagged(moved, last, early, row_norm, blocks):
    rows, time = moved.shape[1:]
    columns = rows * blocks
    width = time // 4
    span = last.shape[0]
    return pl.pallas_call(
        functools.partial(lag_kernel, rows, blocks),
        out_shape=(
            jax.ShapeDtypeStruct((LAGS, rows, columns), jnp.float32),
            jax.ShapeDtypeStruct((rows, width), jnp.bfloat16),
        ),
        grid=(LAGS,),
        in_specs=[
            pl.BlockSpec((1, rows, time), lambda lag: (lag, 0, 0)),
            pl.BlockSpec((span, time), lambda lag: (0, 0)),
            pl.BlockSpec((early.shape[0], 1, rows, span), lambda lag: (0, lag, 0, 0)),
            pl.BlockSpec((rows, 128), lambda lag: (0, 0)),
        ],
        out_specs=(
            pl.BlockSpec((1, rows, columns), lambda lag: (lag, 0, 0)),
            pl.BlockSpec((rows, width), lambda lag: (0, 0)),
        ),
        scratch_shapes=[pltpu.VMEM((8, span), jnp.float32)],
        compiler_params=pltpu.CompilerParams(vmem_limit_bytes=56 * 1024 * 1024),
        cost_estimate=pl.CostEstimate(
            flops=2 * LAGS * rows * span * time,
            bytes_accessed=4 * LAGS * rows * columns,
            transcendentals=LAGS * rows * columns,
        ),
    )(moved, last, early, row_norm)


def shards(raw, taps):
    streams = lax.axis_size("stream")
    blocks = streams // lax.axis_size("tm")
    half = (taps.shape[0] - 1) // 2
    lead = PAD - half
    base = jnp.pad(taps, (lead, WIN - lead - taps.shape[0]))[None, :]
    moved, last, early, row_norm = gather(raw, base, streams, blocks)
    return lagged(moved, last, early, row_norm, blocks)


def solution(mesh):
    placed = (P("stream", "tm"), P())
    return jax.shard_map(
        shards,
        mesh=mesh,
        in_specs=placed,
        out_specs=(P(None, "stream", "tm"), P("stream", "tm")),
        check_vma=False,
    )
```

```python
import functools

import jax
import jax.numpy as jnp
from jax import lax
from jax.experimental import pallas as pl
from jax.experimental.pallas import tpu as pltpu
from jax.sharding import PartitionSpec as P

LAGS = 9
REACH = 4
PAD = 128
OUT = 256
WIN = OUT + 2 * PAD
CHUNK = 16
WIDE = 32
NT = (((1,), (1,)), ((), ()))
MESH = pl.DeviceIdType.MESH


def inverse_norm(wide):
    energy = jnp.sum(wide * wide, axis=1, keepdims=True)
    return 1.0 / jnp.sqrt(1.25 * (energy + 1e-05))


def column_inverse_norms(block):
    pieces = []
    for r in range(block.shape[0] // 128):
        column = inverse_norm(block[128 * r:128 * (r + 1)].astype(jnp.float32))
        pieces.append(jnp.transpose(jnp.broadcast_to(column, (128, 128)))[:8])
    return jnp.concatenate(pieces, axis=1)


def to_information(moments, row_norm, column_norm):
    ratio = moments * row_norm * column_norm
    return -0.5 * jnp.log(1.0 - ratio * ratio)


def group_rows(rows):
    return 256 if rows % 256 == 0 else rows


def gather_kernel(
    streams, blocks, raw_ref, base_ref, moved_out, last_out, early_out, row_ref,
    full, bands, moved, held, stage, column_ref, *sems
):
    p1_send, p1_recv, up_send, down_send, z_recv, x_send, x_recv, stage_sem, moved_sem, last_sem = sems
    rows, width = raw_ref.shape
    time = moved.shape[2]
    layers = streams // blocks
    chunks = rows // CHUNK
    wide_chunks = rows // WIDE
    part = group_rows(rows)
    groups = rows // part
    span = blocks * part
    per_group = part // CHUNK
    dots = LAGS * (groups - 1)
    first_dot = wide_chunks + 2
    s = lax.axis_index("stream")
    t = lax.axis_index("tm")
    z = s // blocks
    g = s % blocks
    source = z == t

    barrier = pltpu.get_barrier_semaphore()

    def greet(target):
        pl.semaphore_signal(barrier, inc=1, device_id=target, device_id_type=MESH)

    def peer_tm(d):
        return (t + d) % 4

    def peer_g(d):
        return z * blocks + (g + d) % blocks

    for d in (1, 2, 3):
        greet({"tm": peer_tm(d)})
    for d in range(1, blocks):
        greet({"stream": peer_g(d)})

    @pl.when(z > 0)
    def _():
        greet({"stream": s - blocks})

    @pl.when(z < layers - 1)
    def _():
        greet({"stream": s + blocks})

    count = 3 + blocks - 1 + jnp.where(z > 0, 1, 0) + jnp.where(z < layers - 1, 1, 0)
    pl.semaphore_wait(barrier, count)

    def wide_rows(f):
        return pl.ds(pl.multiple_of(f * WIDE, WIDE), WIDE)

    def lanes_of(q):
        return pl.ds(pl.multiple_of(PAD + q * width, PAD), width)

    def p1_copy(f, d):
        return pltpu.make_async_remote_copy(
            src_ref=raw_ref.at[wide_rows(f)],
            dst_ref=full.at[wide_rows(f), lanes_of(t)],
            send_sem=p1_send.at[d - 1, f],
            recv_sem=p1_recv.at[d - 1, f],
            device_id={"tm": peer_tm(d)},
            device_id_type=MESH,
        )

    @pl.loop(0, wide_chunks)
    def _(f):
        for d in (2, 3, 1):
            p1_copy(f, d).start()

    full[:, lanes_of(t)] = raw_ref[...]
    full[:, :PAD] = jnp.zeros((rows, PAD), full.dtype)
    full[:, PAD + time:] = jnp.zeros((rows, PAD), full.dtype)
    band = pltpu.roll(jnp.broadcast_to(base_ref[...], (OUT, WIN)), 0, 1, stride=1, stride_axis=0)
    for k in range(3):
        piece = band.astype(jnp.bfloat16)
        bands[k] = piece
        band = band - piece.astype(jnp.float32)

    def held_rows(c, size):
        place = (c // per_group) * span + g * part + (c % per_group) * CHUNK
        return pl.ds(pl.multiple_of(place, CHUNK), size)

    def z_copy(c, step, send):
        return pltpu.make_async_remote_copy(
            src_ref=held.at[held_rows(c, CHUNK)],
            dst_ref=held.at[held_rows(c, CHUNK)],
            send_sem=send.at[c],
            recv_sem=z_recv.at[c],
            device_id={"stream": s + step},
            device_id_type=MESH,
        )

    def x_copy(c, d):
        return pltpu.make_async_remote_copy(
            src_ref=held.at[held_rows(c, CHUNK)],
            dst_ref=held.at[held_rows(c, CHUNK)],
            send_sem=x_send.at[d - 1, c],
            recv_sem=x_recv.at[d - 1, c],
            device_id={"stream": peer_g(d)},
            device_id_type=MESH,
        )

    rising = (z >= t) & (z < layers - 1)
    falling = (z <= t) & (z > 0)

    def forward(c):
        @pl.when(rising)
        def _():
            z_copy(c, blocks, up_send).start()

        @pl.when(falling)
        def _():
            z_copy(c, -blocks, down_send).start()

        for d in range(1, blocks):
            x_copy(c, d).start()

    def filter_rows(f):
        for d in (2, 3, 1):
            p1_copy(f, d).wait_recv()
        here = wide_rows(f)
        stack = jnp.concatenate(
            [full[here, OUT * b:OUT * b + WIN] for b in range(time // OUT)], axis=0
        )
        total = lax.dot_general(stack, bands[2], NT, preferred_element_type=jnp.float32)
        total += lax.dot_general(stack, bands[1], NT, preferred_element_type=jnp.float32)
        total += lax.dot_general(stack, bands[0], NT, preferred_element_type=jnp.float32)
        values = total.astype(jnp.bfloat16)
        for b in range(time // OUT):
            moved[REACH, here, OUT * b:OUT * (b + 1)] = values[WIDE * b:WIDE * (b + 1)]

        @pl.when(source)
        def _():
            there = held_rows(f * (WIDE // CHUNK), WIDE)
            held[there] = moved[REACH, here]
            for u in range(WIDE // CHUNK):
                forward(f * (WIDE // CHUNK) + u)

        wide = moved[REACH, here].astype(jnp.float32)
        row_ref[here] = jnp.broadcast_to(inverse_norm(wide), (WIDE, 128))
        for k in range(LAGS):
            shift = k - REACH
            if shift != 0:
                turned = pltpu.roll(wide, shift % time, 1)
                place = lax.broadcasted_iota(jnp.int32, turned.shape, 1) - shift
                kept = (place >= 0) & (place < time)
                moved[k, here] = jnp.where(kept, turned, 0.0).astype(jnp.bfloat16)

    def moved_copy():
        return pltpu.make_async_copy(moved, moved_out, moved_sem)

    def stage_copy(n):
        return pltpu.make_async_copy(
            stage.at[n % 2], early_out.at[n // LAGS, n % LAGS], stage_sem.at[n % 2]
        )

    def one_dot(n):
        k = n // LAGS
        block = pl.ds(pl.multiple_of(k * span, span), span)

        @pl.when(n % LAGS == 0)
        def _():
            @pl.loop(0, per_group)
            def _(c):
                for d in range(1, blocks):
                    x_copy(k * per_group + c, d).wait_recv()

            column_ref[k] = column_inverse_norms(held[block])

        @pl.when(n >= 2)
        def _():
            stage_copy(n - 2).wait()

        moments = lax.dot_general(
            moved[n % LAGS], held[block], NT, preferred_element_type=jnp.float32
        )
        stage[n % 2] = to_information(moments, row_ref[:, :1], column_ref[k, :1])
        stage_copy(n).start()

    def relayed(c):
        return jnp.where(c < wide_chunks, 3 * c // 2, c + wide_chunks // 2)

    @pl.loop(0, max(chunks, first_dot + dots))
    def _(c):
        @pl.loop(relayed(c), relayed(c + 1))
        def _(q):
            @pl.when(jnp.logical_not(source) & (q < chunks))
            def _():
                z_copy(q, jnp.where(z > t, -blocks, blocks), up_send).wait_recv()
                forward(q)

        @pl.when(c < wide_chunks)
        def _():
            filter_rows(c)

        @pl.when(c == wide_chunks)
        def _():
            moved_copy().start()

        if dots:
            n = c - first_dot

            @pl.when((n >= 0) & (n < dots))
            def _():
                one_dot(n)

    @pl.loop((groups - 1) * per_group, chunks)
    def _(c):
        for d in range(1, blocks):
            x_copy(c, d).wait_recv()

    last = pltpu.make_async_copy(held.at[pl.ds((groups - 1) * span, span)], last_out, last_sem)
    last.start()

    @pl.loop(0, wide_chunks)
    def _(f):
        for d in (1, 2, 3):
            p1_copy(f, d).wait_send()

    @pl.loop(0, chunks)
    def _(c):
        for d in range(1, blocks):
            x_copy(c, d).wait_send()

        @pl.when(rising)
        def _():
            z_copy(c, blocks, up_send).wait_send()

        @pl.when(falling)
        def _():
            z_copy(c, -blocks, down_send).wait_send()

    if dots:
        stage_copy(dots - 2).wait()
        stage_copy(dots - 1).wait()
    moved_copy().wait()
    last.wait()


def gather(raw, base, streams, blocks):
    rows, width = raw.shape
    time = width * 4
    chunks = rows // CHUNK
    part = group_rows(rows)
    span = part * blocks
    early = max(rows // part - 1, 1)
    dma = pltpu.SemaphoreType.DMA
    vmem = pl.BlockSpec(memory_space=pltpu.VMEM)
    anywhere = pl.BlockSpec(memory_space=pl.ANY)
    return pl.pallas_call(
        functools.partial(gather_kernel, streams, blocks),
        out_shape=(
            jax.ShapeDtypeStruct((LAGS, rows, time), jnp.bfloat16),
            jax.ShapeDtypeStruct((span, time), jnp.bfloat16),
            jax.ShapeDtypeStruct((early, LAGS, rows, span), jnp.float32),
            jax.ShapeDtypeStruct((rows, 128), jnp.float32),
        ),
        in_specs=[vmem, vmem],
        out_specs=(anywhere, anywhere, anywhere, vmem),
        scratch_shapes=[
            pltpu.VMEM((rows, time + 2 * PAD), jnp.bfloat16),
            pltpu.VMEM((3, OUT, WIN), jnp.bfloat16),
            pltpu.VMEM((LAGS, rows, time), jnp.bfloat16),
            pltpu.VMEM((rows * blocks, time), jnp.bfloat16),
            pltpu.VMEM((2, rows, span), jnp.float32),
            pltpu.VMEM((early, 8, span), jnp.float32),
            dma((3, rows // WIDE)),
            dma((3, rows // WIDE)),
            dma((chunks,)),
            dma((chunks,)),
            dma((chunks,)),
            dma((max(blocks - 1, 1), chunks)),
            dma((max(blocks - 1, 1), chunks)),
            dma((2,)),
            dma,
            dma,
        ],
        compiler_params=pltpu.CompilerParams(
            collective_id=0, has_side_effects=True, vmem_limit_bytes=60 * 1024 * 1024
        ),
        cost_estimate=pl.CostEstimate(
            flops=2 * LAGS * rows * rows * blocks * time,
            bytes_accessed=2 * rows * time * 8,
            transcendentals=0,
        ),
    )(raw, base)


def lag_kernel(
    rows, blocks, moved_ref, last_ref, early_ref, row_ref, out_ref, filtered_ref, column_norm
):
    part = group_rows(rows)
    groups = rows // part
    width = filtered_ref.shape[1]
    lag = pl.program_id(0)

    @pl.when(lag == 0)
    def _():
        column_norm[...] = column_inverse_norms(last_ref[...])

    @pl.when(lag == REACH)
    def _():
        here = pl.ds(pl.multiple_of(lax.axis_index("tm") * width, width), width)
        filtered_ref[...] = moved_ref[0, :, here]

    def place(k, values):
        if groups == 1:
            out_ref[0] = values
        else:
            for g in range(blocks):
                start = g * rows + k * part
                out_ref[0, :, start:start + part] = values[:, g * part:(g + 1) * part]

    for k in range(groups - 1):
        place(k, early_ref[k, 0])
    moments = lax.dot_general(moved_ref[0], last_ref[...], NT, preferred_element_type=jnp.float32)
    place(groups - 1, to_information(moments, row_ref[:, :1], column_norm[:1]))


def lagged(moved, last, early, row_norm, blocks):
    rows, time = moved.shape[1:]
    columns = rows * blocks
    width = time // 4
    span = last.shape[0]
    return pl.pallas_call(
        functools.partial(lag_kernel, rows, blocks),
        out_shape=(
            jax.ShapeDtypeStruct((LAGS, rows, columns), jnp.float32),
            jax.ShapeDtypeStruct((rows, width), jnp.bfloat16),
        ),
        grid=(LAGS,),
        in_specs=[
            pl.BlockSpec((1, rows, time), lambda lag: (lag, 0, 0)),
            pl.BlockSpec((span, time), lambda lag: (0, 0)),
            pl.BlockSpec((early.shape[0], 1, rows, span), lambda lag: (0, lag, 0, 0)),
            pl.BlockSpec((rows, 128), lambda lag: (0, 0)),
        ],
        out_specs=(
            pl.BlockSpec((1, rows, columns), lambda lag: (lag, 0, 0)),
            pl.BlockSpec((rows, width), lambda lag: (0, 0)),
        ),
        scratch_shapes=[pltpu.VMEM((8, span), jnp.float32)],
        compiler_params=pltpu.CompilerParams(vmem_limit_bytes=56 * 1024 * 1024),
        cost_estimate=pl.CostEstimate(
            flops=2 * LAGS * rows * span * time,
            bytes_accessed=4 * LAGS * rows * columns,
            transcendentals=LAGS * rows * columns,
        ),
    )(moved, last, early, row_norm)


def shards(raw, taps):
    streams = lax.axis_size("stream")
    blocks = streams // lax.axis_size("tm")
    half = (taps.shape[0] - 1) // 2
    lead = PAD - half
    base = jnp.pad(taps, (lead, WIN - lead - taps.shape[0]))[None, :]
    moved, last, early, row_norm = gather(raw, base, streams, blocks)
    return lagged(moved, last, early, row_norm, blocks)


def solution(mesh):
    placed = (P("stream", "tm"), P())
    return jax.shard_map(
        shards,
        mesh=mesh,
        in_specs=placed,
        out_specs=(P(None, "stream", "tm"), P("stream", "tm")),
        check_vma=False,
    )
```
